32 devices in a mesh: shot: 8 (over z, y), recv: 4 (over x, core).
Axes of the slice: x: 2, y: 2, z: 4, core: 2. Of those that a mesh axis runs over, the one named last changes fastest.
Arguments:
- traces: bfloat16 [2, 2, 4096, 4096], P(None, None, 'shot', 'recv'), may hold values from -6 to 6
Outputs:
- multiples: float32 [2, 2, 4096, 4096], P(None, None, 'shot', 'recv')
The draws below stay inside these ranges and needn't reach their ends.
All inputs are finite; a program needn't handle non-finite values.
Results may differ from the reference program's by a relative error of at most 0.0044.
Values may be sent and summed in bfloat16 or wider, within the bound.
A program may use at most 128 MiB of HBM per device.

```python
import jax
import jax.numpy as jnp
from jax import lax

NS = 4096
FREQ = 2


def steps_of(key, shape, cuts, low, high):
    gain = 1.0
    for dim, parts in cuts:
        steps = jax.random.uniform(jax.random.fold_in(jax.random.fold_in(key, 6), dim), (parts,), jnp.float32, low / len(cuts), high / len(cuts))
        gain = gain * jnp.repeat(jnp.exp(steps), shape[dim] // parts).reshape((-1,) + (1,) * (len(shape) - 1 - dim))
    return gain


def gaussian(key, shape, width, limit, split=(), held_as=jnp.bfloat16):
    result = jax.random.normal(key, shape, jnp.float32) * width
    if len(split) > 0:
        result = steps_of(key, shape, split, -0.22, 0.18) * result
    return jnp.clip(result, min=-limit, max=limit).astype(held_as)


def setup_inputs(seed: int = 0) -> dict:
    seeds = jax.random.split(jax.random.key(seed), 2)
    traces = gaussian(seeds[0], (FREQ, 2, NS, NS), 1.0, 6.0, ((2, 8), (3, 4)))
    return dict(traces=traces)


def mirror_average(component):
    summed = component.astype(jnp.float32) + jnp.transpose(component).astype(jnp.float32)
    return (summed * 0.5).astype(jnp.bfloat16)


def per_frequency(freq_data):
    real_avg = mirror_average(freq_data[0])
    imag_avg = mirror_average(freq_data[1])
    real_out = jnp.dot(real_avg, real_avg, preferred_element_type=jnp.float32) - jnp.dot(imag_avg, imag_avg, preferred_element_type=jnp.float32)
    imag_out = jnp.dot(real_avg, imag_avg, preferred_element_type=jnp.float32) + jnp.dot(imag_avg, real_avg, preferred_element_type=jnp.float32)
    scale_factor = jnp.float32(float(NS) ** -0.5)
    return jnp.stack((real_out, imag_out), axis=0) * scale_factor


def reference(traces):
    return lax.map(per_frequency, traces)
```

```python
import functools

import jax
import jax.numpy as jnp
from jax import lax
from jax.experimental import pallas as pl
from jax.experimental.pallas import tpu as pltpu
from jax.sharding import PartitionSpec as P

NS = 4096
MESH = pl.DeviceIdType.MESH
ANY = pl.BlockSpec(memory_space=pl.ANY)


class Place:
    def __init__(self):
        shot, recv = lax.axis_index("shot"), lax.axis_index("recv")
        self.hi, self.zl, self.y = shot // 4, (shot // 2) % 2, shot % 2
        self.x, self.core = recv // 2, recv % 2
        self.row_group = self.zl * 2 + self.y
        self.recv = recv

    def device(self, **moved):
        at = dict(hi=self.hi, zl=self.zl, y=self.y, x=self.x, core=self.core)
        at.update(moved)
        return ((at["hi"] * 2 + at["zl"]) * 2 + at["y"], at["x"] * 2 + at["core"])


def greet(targets):
    barrier = pltpu.get_barrier_semaphore()
    for target in targets:
        pl.semaphore_signal(barrier, inc=1, device_id=target, device_id_type=MESH)
    pl.semaphore_wait(barrier, len(targets))


def exchange_kernel(traces, tile, mirror, local_sems, swap_sems, send_sems, recv_sems):
    me = Place()
    size = traces.shape[2]
    partner = me.device(hi=1 - me.hi)
    blocks = [(flip, col) for flip in range(2) for col in range(2)]

    def half(flip):
        return me.hi if flip == 0 else 1 - me.hi

    def target(flip, col):
        return me.device(zl=me.core, y=col, x=half(flip), core=me.zl)

    def is_self(flip, col):
        return (me.core == me.zl) & (me.y == col) & (me.x == half(flip))

    barrier = pltpu.get_barrier_semaphore()
    pl.semaphore_signal(barrier, inc=1, device_id=partner, device_id_type=MESH)
    for flip, col in blocks:
        @pl.when(jnp.logical_not(is_self(flip, col)))
        def _():
            pl.semaphore_signal(barrier, inc=1, device_id=target(flip, col), device_id_type=MESH)
    self_count = jnp.where((me.core == me.zl), 1, 0)
    pl.semaphore_wait(barrier, 5 - self_count)

    swaps = [
        pltpu.make_async_remote_copy(
            src_ref=traces.at[1 - me.hi, c], dst_ref=tile.at[c, me.hi],
            send_sem=swap_sems.at[0, c], recv_sem=swap_sems.at[1, c],
            device_id=partner, device_id_type=MESH,
        )
        for c in range(2)
    ]
    for swap in swaps:
        swap.start()
    own = pltpu.make_async_copy(traces.at[me.hi], tile.at[:, me.hi], local_sems.at[0])
    own.start()

    def source(flip, col, c):
        columns = pl.ds(col * size, size)
        if flip == 0:
            return traces.at[me.hi, c, :, columns]
        return tile.at[c, 1 - me.hi, :, columns]

    def remote(flip, col, c):
        return pltpu.make_async_remote_copy(
            src_ref=source(flip, col, c), dst_ref=mirror.at[c, me.x, me.y],
            send_sem=send_sems.at[c, half(flip), col], recv_sem=recv_sems.at[c, me.x, me.y],
            device_id=target(flip, col), device_id_type=MESH,
        )

    def local(flip, col, c):
        return pltpu.make_async_copy(
            source(flip, col, c), mirror.at[c, me.x, me.y], local_sems.at[1 + c]
        )

    def begin(flip, c):
        for col in range(2):
            @pl.when(is_self(flip, col))
            def _():
                local(flip, col, c).start()

            @pl.when(jnp.logical_not(is_self(flip, col)))
            def _():
                remote(flip, col, c).start()

    for c in range(2):
        begin(0, c)
    for c in range(2):
        swaps[c].wait_recv()
        begin(1, c)
    own.wait()
    for c in range(2):
        swaps[c].wait_send()
        for flip, col in blocks:
            @pl.when(is_self(flip, col))
            def _():
                local(flip, col, c).wait()

            @pl.when(jnp.logical_not(is_self(flip, col)))
            def _():
                remote(flip, col, c).wait_send()
                pltpu.make_async_remote_copy(
                    src_ref=mirror.at[c, half(flip), col], dst_ref=mirror.at[c, half(flip), col],
                    send_sem=send_sems.at[c, half(flip), col],
                    recv_sem=recv_sems.at[c, half(flip), col],
                    device_id=target(flip, col), device_id_type=MESH,
                ).wait_recv()


def exchange(traces):
    size, width = traces.shape[2:]
    return pl.pallas_call(
        exchange_kernel,
        out_shape=(
            jax.ShapeDtypeStruct((2, 2, size, width), traces.dtype),
            jax.ShapeDtypeStruct((2, 2, 2, size, width // 2), traces.dtype),
        ),
        in_specs=[ANY],
        out_specs=(ANY, ANY),
        scratch_shapes=[
            pltpu.SemaphoreType.DMA((3,)),
            pltpu.SemaphoreType.DMA((2, 2)),
            pltpu.SemaphoreType.DMA((2, 2, 2)),
            pltpu.SemaphoreType.DMA((2, 2, 2)),
        ],
        compiler_params=pltpu.CompilerParams(collective_id=0, has_side_effects=True),
        name="exchange",
    )(traces)


def average_kernel(tile, mirror, out):
    total = tile[0, 0].astype(jnp.float32) + jnp.transpose(mirror[0, 0, 0]).astype(jnp.float32)
    out[0] = (total * 0.5).astype(out.dtype)


def average(tile, mirror):
    size, width = tile.shape[2:]
    return pl.pallas_call(
        average_kernel,
        grid=(2, 2, 2),
        out_shape=jax.ShapeDtypeStruct((2, 2 * size, width), tile.dtype),
        in_specs=[
            pl.BlockSpec((1, 1, size, size), lambda c, h, y: (c, h, 0, y)),
            pl.BlockSpec((1, 1, 1, size, size), lambda c, h, y: (c, h, y, 0, 0)),
        ],
        out_specs=pl.BlockSpec((1, size, size), lambda c, h, y: (c, h, y)),
        compiler_params=pltpu.CompilerParams(vmem_limit_bytes=32 * 2**20),
        name="average",
    )(tile, mirror)


def gather_kernel(mean, rows, cols, local_sems, send_sems, recv_sems):
    me = Place()
    across_x, across_core = me.device(x=1 - me.x), me.device(core=1 - me.core)
    across_y, across_z = me.device(y=1 - me.y), me.device(zl=1 - me.zl)
    greet([across_x, across_core, across_y, across_z])
    mine, group = me.recv, me.row_group
    group_y = me.zl * 2 + 1 - me.y
    group_z = (1 - me.zl) * 2 + me.y
    recv_x = (1 - me.x) * 2 + me.core

    def send(k, source, dest, device):
        return pltpu.make_async_remote_copy(
            src_ref=source, dst_ref=dest, send_sem=send_sems.at[k], recv_sem=recv_sems.at[k],
            device_id=device, device_id_type=MESH,
        )

    copies = [
        send(0, mean.at[0], cols.at[group, 0], across_y),
        send(1, mean.at[1], cols.at[group, 1], across_z),
        send(2, mean, rows.at[mine], across_x),
        send(3, mean, rows.at[mine], across_core),
        send(4, mean.at[1], cols.at[group, 1], across_y),
        send(5, mean.at[0], cols.at[group, 0], across_z),
    ]
    relays = [
        send(6, cols.at[group_y, 0], cols.at[group_y, 0], across_z),
        send(7, cols.at[group_z, 1], cols.at[group_z, 1], across_y),
        send(8, rows.at[recv_x], rows.at[recv_x], across_core),
    ]
    locals_ = [
        pltpu.make_async_copy(mean, cols.at[group], local_sems.at[0]),
        pltpu.make_async_copy(mean, rows.at[mine], local_sems.at[1]),
    ]
    for copy in copies + locals_:
        copy.start()
    for copy, relay in zip(copies, relays):
        copy.wait_recv()
        relay.start()
    for copy in copies[3:] + relays:
        copy.wait_recv()
    for copy in copies + relays:
        copy.wait_send()
    for copy in locals_:
        copy.wait()


def gather(mean):
    panel = jax.ShapeDtypeStruct((4,) + mean.shape, mean.dtype)
    return pl.pallas_call(
        gather_kernel,
        out_shape=(panel, panel),
        in_specs=[ANY],
        out_specs=(ANY, ANY),
        scratch_shapes=[
            pltpu.SemaphoreType.DMA((2,)),
            pltpu.SemaphoreType.DMA((9,)),
            pltpu.SemaphoreType.DMA((9,)),
        ],
        compiler_params=pltpu.CompilerParams(collective_id=1, has_side_effects=True),
        name="gather",
    )(mean)


def product_kernel(scale, rows, cols, out):
    half = rows.shape[2] // 2
    real = imag = None
    for k in range(8):
        left = rows.at[k // 2, :, :, pl.ds((k % 2) * half, half)]
        right = cols.at[k % 4, :, pl.ds((k // 4) * half, half), :]
        dot = functools.partial(jnp.dot, preferred_element_type=jnp.float32)
        re = dot(left[0], right[0]) - dot(left[1], right[1])
        im = dot(left[0], right[1]) + dot(left[1], right[0])
        real, imag = (re, im) if real is None else (real + re, imag + im)
    out[0] = real * scale
    out[1] = imag * scale


def product(rows, cols, tile_cols=256):
    size = rows.shape[2]
    return pl.pallas_call(
        functools.partial(product_kernel, float(NS) ** (-0.5)),
        grid=(size // tile_cols,),
        out_shape=jax.ShapeDtypeStruct((2, size, size), jnp.float32),
        in_specs=[
            pl.BlockSpec(rows.shape, lambda n: (0, 0, 0, 0), pipeline_mode=pl.Buffered(1)),
            pl.BlockSpec((4, 2, size, tile_cols), lambda n: (0, 0, 0, n)),
        ],
        out_specs=pl.BlockSpec((2, size, tile_cols), lambda n: (0, 0, n)),
        compiler_params=pltpu.CompilerParams(vmem_limit_bytes=56 * 2**20),
        cost_estimate=pl.CostEstimate(
            flops=2 * 4 * size * size * 4 * size, bytes_accessed=40 * 2**20, transcendentals=0
        ),
        name="product",
    )(rows, cols)


def cube_per_device(traces):
    size = traces.shape[2]
    hi = lax.axis_index("shot") // 4
    mean = average(*exchange(traces))
    result = product(*gather(mean)).reshape(2, 2, size, 2 * size)
    kept = lax.dynamic_index_in_dim(result, hi, 1, keepdims=False)
    sent = lax.dynamic_index_in_dim(result, 1 - hi, 1, keepdims=False).astype(jnp.bfloat16)
    got = lax.ppermute(sent, "shot", [(s, (s + 4) % 8) for s in range(8)]).astype(jnp.float32)
    first = hi == 0
    return jnp.stack((jnp.where(first, kept, got), jnp.where(first, got, kept)))


def complex_product(left_block, right_block, form):
    real_real = jnp.einsum(
        form, left_block[:, 0], right_block[:, 0], preferred_element_type=jnp.float32
    )
    imag_imag = jnp.einsum(
        form, left_block[:, 1], right_block[:, 1], preferred_element_type=jnp.float32
    )
    real_imag = jnp.einsum(
        form, left_block[:, 0], right_block[:, 1], preferred_element_type=jnp.float32
    )
    imag_real = jnp.einsum(
        form, left_block[:, 1], right_block[:, 0], preferred_element_type=jnp.float32
    )
    return jnp.stack((real_real - imag_imag, real_imag + imag_real), axis=1)


def per_device(traces):
    freqs = traces.shape[0]
    block_rows = traces.shape[2]
    col_width = traces.shape[3]
    recv_count = lax.axis_size("recv")
    shot_count = lax.axis_size("shot")
    group_blocks = shot_count // recv_count
    piece_len = block_rows // recv_count
    total = shot_count * block_rows
    row_split = traces.reshape(freqs, 2, recv_count, piece_len, col_width)
    col_split = traces.reshape(freqs, 2, block_rows, group_blocks, recv_count, piece_len)
    col_split = jnp.transpose(col_split, (0, 1, 4, 2, 3, 5))
    got_rows, got_cols = (
        lax.all_to_all(row_split, "recv", split_axis=2, concat_axis=2, tiled=True),
        lax.all_to_all(col_split, "recv", split_axis=2, concat_axis=2, tiled=True),
    )
    wide_rows = jnp.transpose(got_rows, (0, 1, 3, 2, 4)).reshape(freqs, 2, piece_len, total)
    own_cols = jnp.transpose(got_cols, (0, 1, 3, 2, 4, 5)).reshape(freqs, 2, block_rows, col_width)
    mirrored = lax.all_to_all(wide_rows, "shot", split_axis=3, concat_axis=2, tiled=True)
    summed = own_cols.astype(jnp.float32) + jnp.swapaxes(mirrored, 2, 3).astype(jnp.float32)
    averaged = (summed * 0.5).astype(jnp.bfloat16)
    spread = lax.all_gather(averaged, "recv", axis=3, tiled=True)
    spread = spread.reshape(freqs, 2, block_rows, recv_count, shot_count, piece_len)
    panel = jnp.transpose(spread, (0, 1, 2, 4, 3, 5)).reshape(freqs, 2, block_rows, total)
    recv_index = lax.axis_index("recv")
    own_tile = lax.dynamic_slice_in_dim(panel, recv_index * col_width, col_width, 3)
    product = complex_product(
        panel, lax.all_gather(own_tile, "shot", axis=2, tiled=True), "fik,fkj->fij"
    )
    scale_factor = jnp.float32(float(NS) ** (-0.5))
    return product * scale_factor


def solution(mesh):
    placed = (P(None, None, "shot", "recv"),)
    fits = mesh.shape["shot"] == 8 and mesh.shape["recv"] == 4
    return jax.shard_map(
        cube_per_device if fits else per_device,
        mesh=mesh,
        in_specs=placed,
        out_specs=P(None, None, "shot", "recv"),
        check_vma=False,
    )
```

```python
import functools

import jax
import jax.numpy as jnp
from jax import lax
from jax.experimental import pallas as pl
from jax.experimental.pallas import tpu as pltpu
from jax.sharding import PartitionSpec as P

NS = 4096
MESH = pl.DeviceIdType.MESH
ANY = pl.BlockSpec(memory_space=pl.ANY)


class Place:
    def __init__(self):
        shot, recv = lax.axis_index("shot"), lax.axis_index("recv")
        self.hi, self.zl, self.y = shot // 4, (shot // 2) % 2, shot % 2
        self.x, self.core = recv // 2, recv % 2
        self.row_group = self.zl * 2 + self.y
        self.recv = recv

    def device(self, **moved):
        at = dict(hi=self.hi, zl=self.zl, y=self.y, x=self.x, core=self.core)
        at.update(moved)
        return ((at["hi"] * 2 + at["zl"]) * 2 + at["y"], at["x"] * 2 + at["core"])


def greet(targets):
    barrier = pltpu.get_barrier_semaphore()
    for target in targets:
        pl.semaphore_signal(barrier, inc=1, device_id=target, device_id_type=MESH)
    pl.semaphore_wait(barrier, len(targets))


def exchange_kernel(traces, tile, mirror, local_sems, swap_sems, send_sems, recv_sems):
    me = Place()
    size = traces.shape[2]
    partner = me.device(hi=1 - me.hi)
    blocks = [(flip, col) for flip in range(2) for col in range(2)]

    def half(flip):
        return me.hi if flip == 0 else 1 - me.hi

    def target(flip, col):
        return me.device(zl=me.core, y=col, x=half(flip), core=me.zl)

    def is_self(flip, col):
        return (me.core == me.zl) & (me.y == col) & (me.x == half(flip))

    barrier = pltpu.get_barrier_semaphore()
    pl.semaphore_signal(barrier, inc=1, device_id=partner, device_id_type=MESH)
    for flip, col in blocks:
        @pl.when(jnp.logical_not(is_self(flip, col)))
        def _():
            pl.semaphore_signal(barrier, inc=1, device_id=target(flip, col), device_id_type=MESH)
    self_count = jnp.where((me.core == me.zl), 1, 0)
    pl.semaphore_wait(barrier, 5 - self_count)

    swaps = [
        pltpu.make_async_remote_copy(
            src_ref=traces.at[1 - me.hi, c], dst_ref=tile.at[c, me.hi],
            send_sem=swap_sems.at[0, c], recv_sem=swap_sems.at[1, c],
            device_id=partner, device_id_type=MESH,
        )
        for c in range(2)
    ]
    for swap in swaps:
        swap.start()
    own = pltpu.make_async_copy(traces.at[me.hi], tile.at[:, me.hi], local_sems.at[0])
    own.start()

    def source(flip, col, c):
        columns = pl.ds(col * size, size)
        if flip == 0:
            return traces.at[me.hi, c, :, columns]
        return tile.at[c, 1 - me.hi, :, columns]

    def remote(flip, col, c):
        return pltpu.make_async_remote_copy(
            src_ref=source(flip, col, c), dst_ref=mirror.at[c, me.x, me.y],
            send_sem=send_sems.at[c, half(flip), col], recv_sem=recv_sems.at[c, me.x, me.y],
            device_id=target(flip, col), device_id_type=MESH,
        )

    def local(flip, col, c):
        return pltpu.make_async_copy(
            source(flip, col, c), mirror.at[c, me.x, me.y], local_sems.at[1 + c]
        )

    def begin(flip, c):
        for col in range(2):
            @pl.when(is_self(flip, col))
            def _():
                local(flip, col, c).start()

            @pl.when(jnp.logical_not(is_self(flip, col)))
            def _():
                remote(flip, col, c).start()

    for c in range(2):
        begin(0, c)
    for c in range(2):
        swaps[c].wait_recv()
        begin(1, c)
    own.wait()
    for c in range(2):
        swaps[c].wait_send()
        for flip, col in blocks:
            @pl.when(is_self(flip, col))
            def _():
                local(flip, col, c).wait()

            @pl.when(jnp.logical_not(is_self(flip, col)))
            def _():
                remote(flip, col, c).wait_send()
                pltpu.make_async_remote_copy(
                    src_ref=mirror.at[c, half(flip), col], dst_ref=mirror.at[c, half(flip), col],
                    send_sem=send_sems.at[c, half(flip), col],
                    recv_sem=recv_sems.at[c, half(flip), col],
                    device_id=target(flip, col), device_id_type=MESH,
                ).wait_recv()


def exchange(traces):
    size, width = traces.shape[2:]
    return pl.pallas_call(
        exchange_kernel,
        out_shape=(
            jax.ShapeDtypeStruct((2, 2, size, width), traces.dtype),
            jax.ShapeDtypeStruct((2, 2, 2, size, width // 2), traces.dtype),
        ),
        in_specs=[ANY],
        out_specs=(ANY, ANY),
        scratch_shapes=[
            pltpu.SemaphoreType.DMA((3,)),
            pltpu.SemaphoreType.DMA((2, 2)),
            pltpu.SemaphoreType.DMA((2, 2, 2)),
            pltpu.SemaphoreType.DMA((2, 2, 2)),
        ],
        compiler_params=pltpu.CompilerParams(collective_id=0, has_side_effects=True),
        name="exchange",
    )(traces)


def average_kernel(tile, mirror, out):
    total = tile[0, 0].astype(jnp.float32) + jnp.transpose(mirror[0, 0, 0]).astype(jnp.float32)
    out[0] = (total * 0.5).astype(out.dtype)


def average(tile, mirror):
    size, width = tile.shape[2:]
    return pl.pallas_call(
        average_kernel,
        grid=(2, 2, 2),
        out_shape=jax.ShapeDtypeStruct((2, 2 * size, width), tile.dtype),
        in_specs=[
            pl.BlockSpec((1, 1, size, size), lambda c, h, y: (c, h, 0, y)),
            pl.BlockSpec((1, 1, 1, size, size), lambda c, h, y: (c, h, y, 0, 0)),
        ],
        out_specs=pl.BlockSpec((1, size, size), lambda c, h, y: (c, h, y)),
        compiler_params=pltpu.CompilerParams(vmem_limit_bytes=32 * 2**20),
        name="average",
    )(tile, mirror)


def multiply_kernel(chunks, scale, mean, kept, got, rows, cols, home, acc, local_sems, send_sems, recv_sems):
    me = Place()
    size = mean.shape[1] // 2
    width = mean.shape[2]
    wide = width // chunks
    across_x, across_core = me.device(x=1 - me.x), me.device(core=1 - me.core)
    across_y, across_z = me.device(y=1 - me.y), me.device(zl=1 - me.zl)
    partner = me.device(hi=1 - me.hi)
    greet([across_x, across_core, across_y, across_z, partner])
    mine, group = me.recv, me.row_group
    group_y = me.zl * 2 + 1 - me.y
    group_z = (1 - me.zl) * 2 + me.y
    recv_x = (1 - me.x) * 2 + me.core
    count = [0]

    def remote(source, dest, device):
        k = count[0]
        count[0] += 1
        return pltpu.make_async_remote_copy(
            src_ref=source, dst_ref=dest, send_sem=send_sems.at[k], recv_sem=recv_sems.at[k],
            device_id=device, device_id_type=MESH,
        )

    def half(flip):
        return pl.ds(pl.multiple_of((1 - me.hi if flip == 0 else me.hi) * size, size), size)

    def part(j):
        return pl.ds(j * wide, wide)

    started = []

    def start(*copies):
        for copy in copies:
            copy.start()
            started.append(copy)

    def arrive(*copies):
        for copy in copies:
            copy.wait_recv()

    def own(j, c, device):
        return remote(mean.at[c, :, part(j)], cols.at[group, c, :, part(j)], device)

    def relay(j, c, origin, device):
        piece = cols.at[origin, c, :, part(j)]
        return remote(piece, piece, device)

    y_own = [[own(j, c, across_y) for c in range(2)] for j in range(chunks)]
    z_own = [[own(j, c, across_z) for c in range(2)] for j in range(chunks)]
    relays = [
        [
            relay(j, 0, group_y, across_z) if 2 * j < chunks else relay(j, 0, group_z, across_y),
            relay(j, 1, group_z, across_y),
        ]
        for j in range(chunks)
    ]
    row_x = [remote(mean.at[:, half(f)], rows.at[mine, :, half(f)], across_x) for f in range(2)]
    row_core = [remote(mean.at[:, half(f)], rows.at[mine, :, half(f)], across_core) for f in range(2)]
    row_relay = [
        remote(rows.at[recv_x, :, half(f)], rows.at[recv_x, :, half(f)], across_core)
        for f in range(2)
    ]
    homes = [
        remote(home.at[:, :, part(j)], got.at[:, :, part(j)], partner) for j in range(chunks)
    ]

    def send_own(j):
        start(y_own[j][0], z_own[j][1], z_own[j][0], y_own[j][1])

    send_own(0)
    start(row_x[0], row_core[0])
    locals_ = [
        pltpu.make_async_copy(mean, rows.at[mine], local_sems.at[0]),
        pltpu.make_async_copy(mean, cols.at[group], local_sems.at[1]),
    ]
    for copy in locals_:
        copy.start()
    start(row_x[1], row_core[1])

    def multiply(flip, columns):
        acc[...] = jnp.zeros_like(acc)

        @pl.loop(0, 4)
        def _(r):
            for y in range(2):
                left = rows.at[r, :, half(flip), pl.ds(y * size, size)]
                depth = pl.ds(pl.multiple_of((r // 2) * size, size), size)
                right = cols.at[(r % 2) * 2 + y, :, depth, columns]
                dot = functools.partial(jnp.dot, preferred_element_type=jnp.float32)
                acc[0] += dot(left[0], right[0]) - dot(left[1], right[1])
                acc[1] += dot(left[0], right[1]) + dot(left[1], right[0])

    def keep(first, last):
        @pl.loop(first, last)
        def _(j):
            columns = pl.ds(pl.multiple_of(j * wide, wide), wide)
            multiply(1, columns)
            kept[:, :, columns] = acc[...] * scale

    for j in range(chunks):
        first_relay, second_relay = relays[j]
        if 2 * j < chunks:
            arrive(y_own[j][0])
            start(first_relay)
            arrive(z_own[j][1])
            start(second_relay)
            rest = [y_own[j][1], z_own[j][0]]
        else:
            arrive(z_own[j][1])
            start(second_relay)
            arrive(z_own[j][0])
            start(first_relay)
            rest = y_own[j]
        if j + 1 < chunks:
            send_own(j + 1)
        if j == 0:
            arrive(row_x[0])
            start(row_relay[0])
            for copy in locals_:
                copy.wait()
            arrive(row_core[0])
        if j == chunks // 2:
            arrive(row_x[1])
            start(row_relay[1])
            arrive(row_core[1])
        arrive(*rest)
        arrive(first_relay, second_relay)
        if j == 0:
            arrive(row_relay[0])
        multiply(0, part(j))
        home[:, :, part(j)] = (acc[...] * scale).astype(home.dtype)
        start(homes[j])
        if j == chunks // 2:
            arrive(row_relay[1])
            keep(0, j)
    keep(chunks // 2, chunks)
    arrive(*homes)
    for copy in started:
        copy.wait_send()


def multiply(mean, chunks=4):
    height, width = mean.shape[1:]
    size = height // 2
    copies = 7 * chunks + 6
    return pl.pallas_call(
        functools.partial(multiply_kernel, chunks, float(NS) ** (-0.5)),
        out_shape=(
            jax.ShapeDtypeStruct((2, size, width), jnp.float32),
            jax.ShapeDtypeStruct((2, size, width), mean.dtype),
        ),
        in_specs=[ANY],
        out_specs=(pl.BlockSpec(memory_space=pltpu.VMEM), ANY),
        scratch_shapes=[
            pltpu.VMEM((4,) + mean.shape, mean.dtype),
            pltpu.VMEM((4,) + mean.shape, mean.dtype),
            pltpu.VMEM((2, size, width), mean.dtype),
            pltpu.VMEM((2, size, width // chunks), jnp.float32),
            pltpu.SemaphoreType.DMA((2,)),
            pltpu.SemaphoreType.DMA((copies,)),
            pltpu.SemaphoreType.DMA((copies,)),
        ],
        compiler_params=pltpu.CompilerParams(
            collective_id=1, has_side_effects=True, vmem_limit_bytes=52 * 2**20
        ),
        cost_estimate=pl.CostEstimate(
            flops=2 * 4 * height * width * 4 * width, bytes_accessed=16 * 2**20, transcendentals=0
        ),
        name="multiply",
    )(mean)


def cube_per_device(traces):
    kept, got = multiply(average(*exchange(traces)))
    first = lax.axis_index("shot") // 4 == 0
    got = got.astype(jnp.float32)
    return jnp.stack((jnp.where(first, kept, got), jnp.where(first, got, kept)))


def complex_product(left_block, right_block, form):
    real_real = jnp.einsum(
        form, left_block[:, 0], right_block[:, 0], preferred_element_type=jnp.float32
    )
    imag_imag = jnp.einsum(
        form, left_block[:, 1], right_block[:, 1], preferred_element_type=jnp.float32
    )
    real_imag = jnp.einsum(
        form, left_block[:, 0], right_block[:, 1], preferred_element_type=jnp.float32
    )
    imag_real = jnp.einsum(
        form, left_block[:, 1], right_block[:, 0], preferred_element_type=jnp.float32
    )
    return jnp.stack((real_real - imag_imag, real_imag + imag_real), axis=1)


def per_device(traces):
    freqs = traces.shape[0]
    block_rows = traces.shape[2]
    col_width = traces.shape[3]
    recv_count = lax.axis_size("recv")
    shot_count = lax.axis_size("shot")
    group_blocks = shot_count // recv_count
    piece_len = block_rows // recv_count
    total = shot_count * block_rows
    row_split = traces.reshape(freqs, 2, recv_count, piece_len, col_width)
    col_split = traces.reshape(freqs, 2, block_rows, group_blocks, recv_count, piece_len)
    col_split = jnp.transpose(col_split, (0, 1, 4, 2, 3, 5))
    got_rows, got_cols = (
        lax.all_to_all(row_split, "recv", split_axis=2, concat_axis=2, tiled=True),
        lax.all_to_all(col_split, "recv", split_axis=2, concat_axis=2, tiled=True),
    )
    wide_rows = jnp.transpose(got_rows, (0, 1, 3, 2, 4)).reshape(freqs, 2, piece_len, total)
    own_cols = jnp.transpose(got_cols, (0, 1, 3, 2, 4, 5)).reshape(freqs, 2, block_rows, col_width)
    mirrored = lax.all_to_all(wide_rows, "shot", split_axis=3, concat_axis=2, tiled=True)
    summed = own_cols.astype(jnp.float32) + jnp.swapaxes(mirrored, 2, 3).astype(jnp.float32)
    averaged = (summed * 0.5).astype(jnp.bfloat16)
    spread = lax.all_gather(averaged, "recv", axis=3, tiled=True)
    spread = spread.reshape(freqs, 2, block_rows, recv_count, shot_count, piece_len)
    panel = jnp.transpose(spread, (0, 1, 2, 4, 3, 5)).reshape(freqs, 2, block_rows, total)
    recv_index = lax.axis_index("recv")
    own_tile = lax.dynamic_slice_in_dim(panel, recv_index * col_width, col_width, 3)
    product = complex_product(
        panel, lax.all_gather(own_tile, "shot", axis=2, tiled=True), "fik,fkj->fij"
    )
    scale_factor = jnp.float32(float(NS) ** (-0.5))
    return product * scale_factor


def solution(mesh):
    placed = (P(None, None, "shot", "recv"),)
    fits = mesh.shape["shot"] == 8 and mesh.shape["recv"] == 4
    return jax.shard_map(
        cube_per_device if fits else per_device,
        mesh=mesh,
        in_specs=placed,
        out_specs=P(None, None, "shot", "recv"),
        check_vma=False,
    )
```

```python
import functools

import jax
import jax.numpy as jnp
from jax import lax
from jax.experimental import pallas as pl
from jax.experimental.pallas import tpu as pltpu
from jax.sharding import PartitionSpec as P

NS = 4096
MESH = pl.DeviceIdType.MESH
ANY = pl.BlockSpec(memory_space=pl.ANY)


class Place:
    def __init__(self):
        shot, recv = lax.axis_index("shot"), lax.axis_index("recv")
        self.hi, self.zl, self.y = shot // 4, (shot // 2) % 2, shot % 2
        self.x, self.core = recv // 2, recv % 2
        self.row_group = self.zl * 2 + self.y
        self.recv = recv

    def device(self, **moved):
        at = dict(hi=self.hi, zl=self.zl, y=self.y, x=self.x, core=self.core)
        at.update(moved)
        return ((at["hi"] * 2 + at["zl"]) * 2 + at["y"], at["x"] * 2 + at["core"])


def greet(targets):
    barrier = pltpu.get_barrier_semaphore()
    for target in targets:
        pl.semaphore_signal(barrier, inc=1, device_id=target, device_id_type=MESH)
    pl.semaphore_wait(barrier, len(targets))


def exchange_kernel(traces, tile, mirror, local_sems, swap_sems, send_sems, recv_sems):
    me = Place()
    size = traces.shape[2]
    pieces = 4

    def at(i):
        return i // 2, pl.ds((i % 2) * (size // 2), size // 2)

    partner = me.device(hi=1 - me.hi)
    blocks = [(flip, col) for flip in range(2) for col in range(2)]

    def half(flip):
        return me.hi if flip == 0 else 1 - me.hi

    def target(flip, col):
        return me.device(zl=me.core, y=col, x=half(flip), core=me.zl)

    def is_self(flip, col):
        return (me.core == me.zl) & (me.y == col) & (me.x == half(flip))

    barrier = pltpu.get_barrier_semaphore()
    pl.semaphore_signal(barrier, inc=1, device_id=partner, device_id_type=MESH)
    for flip, col in blocks:
        @pl.when(jnp.logical_not(is_self(flip, col)))
        def _():
            pl.semaphore_signal(barrier, inc=1, device_id=target(flip, col), device_id_type=MESH)
    self_count = jnp.where((me.core == me.zl), 1, 0)
    pl.semaphore_wait(barrier, 5 - self_count)

    swaps = [
        pltpu.make_async_remote_copy(
            src_ref=traces.at[(1 - me.hi, *at(c))], dst_ref=tile.at[at(c)[0], me.hi, at(c)[1]],
            send_sem=swap_sems.at[0, c], recv_sem=swap_sems.at[1, c],
            device_id=partner, device_id_type=MESH,
        )
        for c in range(pieces)
    ]
    for swap in swaps:
        swap.start()
    own = pltpu.make_async_copy(traces.at[me.hi], tile.at[:, me.hi], local_sems.at[0])
    own.start()

    def source(flip, col, c):
        columns = pl.ds(col * size, size)
        if flip == 0:
            return traces.at[(me.hi, *at(c), columns)]
        return tile.at[at(c)[0], 1 - me.hi, at(c)[1], columns]

    def remote(flip, col, c):
        return pltpu.make_async_remote_copy(
            src_ref=source(flip, col, c), dst_ref=mirror.at[at(c)[0], me.x, me.y, at(c)[1]],
            send_sem=send_sems.at[c, half(flip), col], recv_sem=recv_sems.at[c, me.x, me.y],
            device_id=target(flip, col), device_id_type=MESH,
        )

    def local(flip, col, c):
        return pltpu.make_async_copy(
            source(flip, col, c), mirror.at[at(c)[0], me.x, me.y, at(c)[1]], local_sems.at[1 + c]
        )

    def begin(flip, c):
        for col in range(2):
            @pl.when(is_self(flip, col))
            def _():
                local(flip, col, c).start()

            @pl.when(jnp.logical_not(is_self(flip, col)))
            def _():
                remote(flip, col, c).start()

    for c in range(pieces):
        begin(0, c)
    for c in range(pieces):
        swaps[c].wait_recv()
        begin(1, c)
    own.wait()
    for c in range(pieces):
        swaps[c].wait_send()
        for flip, col in blocks:
            @pl.when(is_self(flip, col))
            def _():
                local(flip, col, c).wait()

            @pl.when(jnp.logical_not(is_self(flip, col)))
            def _():
                remote(flip, col, c).wait_send()
                pltpu.make_async_remote_copy(
                    src_ref=mirror.at[at(c)[0], half(flip), col, at(c)[1]], dst_ref=mirror.at[at(c)[0], half(flip), col, at(c)[1]],
                    send_sem=send_sems.at[c, half(flip), col],
                    recv_sem=recv_sems.at[c, half(flip), col],
                    device_id=target(flip, col), device_id_type=MESH,
                ).wait_recv()


def exchange(traces):
    size, width = traces.shape[2:]
    return pl.pallas_call(
        exchange_kernel,
        out_shape=(
            jax.ShapeDtypeStruct((2, 2, size, width), traces.dtype),
            jax.ShapeDtypeStruct((2, 2, 2, size, width // 2), traces.dtype),
        ),
        in_specs=[ANY],
        out_specs=(ANY, ANY),
        scratch_shapes=[
            pltpu.SemaphoreType.DMA((5,)),
            pltpu.SemaphoreType.DMA((2, 4)),
            pltpu.SemaphoreType.DMA((4, 2, 2)),
            pltpu.SemaphoreType.DMA((4, 2, 2)),
        ],
        compiler_params=pltpu.CompilerParams(collective_id=0, has_side_effects=True),
        name="exchange",
    )(traces)


def average_kernel(tile, mirror, out):
    total = tile[0, 0].astype(jnp.float32) + jnp.transpose(mirror[0, 0, 0]).astype(jnp.float32)
    out[0] = (total * 0.5).astype(out.dtype)


def average(tile, mirror):
    size, width = tile.shape[2:]
    return pl.pallas_call(
        average_kernel,
        grid=(2, 2, 2),
        out_shape=jax.ShapeDtypeStruct((2, 2 * size, width), tile.dtype),
        in_specs=[
            pl.BlockSpec((1, 1, size, size), lambda c, h, y: (c, h, 0, y)),
            pl.BlockSpec((1, 1, 1, size, size), lambda c, h, y: (c, h, y, 0, 0)),
        ],
        out_specs=pl.BlockSpec((1, size, size), lambda c, h, y: (c, h, y)),
        compiler_params=pltpu.CompilerParams(vmem_limit_bytes=32 * 2**20),
        name="average",
    )(tile, mirror)


def multiply_kernel(chunks, scale, mean, kept, got, rows, cols, home, acc, local_sems, send_sems, recv_sems):
    me = Place()
    size = mean.shape[1] // 2
    width = mean.shape[2]
    wide = width // chunks
    across_x, across_core = me.device(x=1 - me.x), me.device(core=1 - me.core)
    across_y, across_z = me.device(y=1 - me.y), me.device(zl=1 - me.zl)
    partner = me.device(hi=1 - me.hi)
    greet([across_x, across_core, across_y, across_z, partner])
    mine, group = me.recv, me.row_group
    group_y = me.zl * 2 + 1 - me.y
    group_z = (1 - me.zl) * 2 + me.y
    recv_x = (1 - me.x) * 2 + me.core
    count = [0]

    def remote(source, dest, device):
        k = count[0]
        count[0] += 1
        return pltpu.make_async_remote_copy(
            src_ref=source, dst_ref=dest, send_sem=send_sems.at[k], recv_sem=recv_sems.at[k],
            device_id=device, device_id_type=MESH,
        )

    def half(flip):
        return pl.ds(pl.multiple_of((1 - me.hi if flip == 0 else me.hi) * size, size), size)

    def part(j):
        return pl.ds(j * wide, wide)

    started = []

    def start(*copies):
        for copy in copies:
            copy.start()
            started.append(copy)

    def arrive(*copies):
        for copy in copies:
            copy.wait_recv()

    def own(j, c, device):
        return remote(mean.at[c, :, part(j)], cols.at[group, c, :, part(j)], device)

    def relay(j, c, origin, device):
        piece = cols.at[origin, c, :, part(j)]
        return remote(piece, piece, device)

    y_own = [[own(j, c, across_y) for c in range(2)] for j in range(chunks)]
    z_own = [[own(j, c, across_z) for c in range(2)] for j in range(chunks)]
    relays = [
        [
            relay(j, 0, group_y, across_z) if 2 * j < chunks else relay(j, 0, group_z, across_y),
            relay(j, 1, group_z, across_y),
        ]
        for j in range(chunks)
    ]
    row_x = [remote(mean.at[:, half(f)], rows.at[mine, :, half(f)], across_x) for f in range(2)]
    row_core = [remote(mean.at[:, half(f)], rows.at[mine, :, half(f)], across_core) for f in range(2)]
    row_relay = [
        remote(rows.at[recv_x, :, half(f)], rows.at[recv_x, :, half(f)], across_core)
        for f in range(2)
    ]
    homes = [
        remote(home.at[:, :, part(j)], got.at[:, :, part(j)], partner) for j in range(chunks)
    ]

    def send_own(j):
        start(y_own[j][0], z_own[j][1], z_own[j][0], y_own[j][1])

    send_own(0)
    start(row_x[0], row_core[0])
    locals_ = [
        pltpu.make_async_copy(mean, rows.at[mine], local_sems.at[0]),
        pltpu.make_async_copy(mean, cols.at[group], local_sems.at[1]),
    ]
    for copy in locals_:
        copy.start()
    start(row_x[1], row_core[1])

    def multiply(flip, columns):
        acc[...] = jnp.zeros_like(acc)

        @pl.loop(0, 4)
        def _(r):
            for y in range(2):
                left = rows.at[r, :, half(flip), pl.ds(y * size, size)]
                depth = pl.ds(pl.multiple_of((r // 2) * size, size), size)
                right = cols.at[(r % 2) * 2 + y, :, depth, columns]
                dot = functools.partial(jnp.dot, preferred_element_type=jnp.float32)
                acc[0] += dot(left[0], right[0]) - dot(left[1], right[1])
                acc[1] += dot(left[0], right[1]) + dot(left[1], right[0])

    def keep(first, last):
        @pl.loop(first, last)
        def _(j):
            columns = pl.ds(pl.multiple_of(j * wide, wide), wide)
            multiply(1, columns)
            kept[:, :, columns] = acc[...] * scale

    for j in range(chunks):
        first_relay, second_relay = relays[j]
        if 2 * j < chunks:
            arrive(y_own[j][0])
            start(first_relay)
            arrive(z_own[j][1])
            start(second_relay)
            rest = [y_own[j][1], z_own[j][0]]
        else:
            arrive(z_own[j][1])
            start(second_relay)
            arrive(z_own[j][0])
            start(first_relay)
            rest = y_own[j]
        if j + 1 < chunks:
            send_own(j + 1)
        if j == 0:
            arrive(row_x[0])
            start(row_relay[0])
            for copy in locals_:
                copy.wait()
            arrive(row_core[0])
        if j == chunks // 2:
            arrive(row_x[1])
            start(row_relay[1])
            arrive(row_core[1])
        arrive(*rest)
        arrive(first_relay, second_relay)
        if j == 0:
            arrive(row_relay[0])
        multiply(0, part(j))
        home[:, :, part(j)] = (acc[...] * scale).astype(home.dtype)
        start(homes[j])
        if j == chunks // 2:
            arrive(row_relay[1])
            keep(0, j)
    keep(chunks // 2, chunks)
    arrive(*homes)
    for copy in started:
        copy.wait_send()


def multiply(mean, chunks=4):
    height, width = mean.shape[1:]
    size = height // 2
    copies = 7 * chunks + 6
    return pl.pallas_call(
        functools.partial(multiply_kernel, chunks, float(NS) ** (-0.5)),
        out_shape=(
            jax.ShapeDtypeStruct((2, size, width), jnp.float32),
            jax.ShapeDtypeStruct((2, size, width), mean.dtype),
        ),
        in_specs=[ANY],
        out_specs=(pl.BlockSpec(memory_space=pltpu.VMEM), ANY),
        scratch_shapes=[
            pltpu.VMEM((4,) + mean.shape, mean.dtype),
            pltpu.VMEM((4,) + mean.shape, mean.dtype),
            pltpu.VMEM((2, size, width), mean.dtype),
            pltpu.VMEM((2, size, width // chunks), jnp.float32),
            pltpu.SemaphoreType.DMA((2,)),
            pltpu.SemaphoreType.DMA((copies,)),
            pltpu.SemaphoreType.DMA((copies,)),
        ],
        compiler_params=pltpu.CompilerParams(
            collective_id=1, has_side_effects=True, vmem_limit_bytes=52 * 2**20
        ),
        cost_estimate=pl.CostEstimate(
            flops=2 * 4 * height * width * 4 * width, bytes_accessed=16 * 2**20, transcendentals=0
        ),
        name="multiply",
    )(mean)


def cube_per_device(traces):
    kept, got = multiply(average(*exchange(traces)))
    first = lax.axis_index("shot") // 4 == 0
    got = got.astype(jnp.float32)
    return jnp.stack((jnp.where(first, kept, got), jnp.where(first, got, kept)))


def complex_product(left_block, right_block, form):
    real_real = jnp.einsum(
        form, left_block[:, 0], right_block[:, 0], preferred_element_type=jnp.float32
    )
    imag_imag = jnp.einsum(
        form, left_block[:, 1], right_block[:, 1], preferred_element_type=jnp.float32
    )
    real_imag = jnp.einsum(
        form, left_block[:, 0], right_block[:, 1], preferred_element_type=jnp.float32
    )
    imag_real = jnp.einsum(
        form, left_block[:, 1], right_block[:, 0], preferred_element_type=jnp.float32
    )
    return jnp.stack((real_real - imag_imag, real_imag + imag_real), axis=1)


def per_device(traces):
    freqs = traces.shape[0]
    block_rows = traces.shape[2]
    col_width = traces.shape[3]
    recv_count = lax.axis_size("recv")
    shot_count = lax.axis_size("shot")
    group_blocks = shot_count // recv_count
    piece_len = block_rows // recv_count
    total = shot_count * block_rows
    row_split = traces.reshape(freqs, 2, recv_count, piece_len, col_width)
    col_split = traces.reshape(freqs, 2, block_rows, group_blocks, recv_count, piece_len)
    col_split = jnp.transpose(col_split, (0, 1, 4, 2, 3, 5))
    got_rows, got_cols = (
        lax.all_to_all(row_split, "recv", split_axis=2, concat_axis=2, tiled=True),
        lax.all_to_all(col_split, "recv", split_axis=2, concat_axis=2, tiled=True),
    )
    wide_rows = jnp.transpose(got_rows, (0, 1, 3, 2, 4)).reshape(freqs, 2, piece_len, total)
    own_cols = jnp.transpose(got_cols, (0, 1, 3, 2, 4, 5)).reshape(freqs, 2, block_rows, col_width)
    mirrored = lax.all_to_all(wide_rows, "shot", split_axis=3, concat_axis=2, tiled=True)
    summed = own_cols.astype(jnp.float32) + jnp.swapaxes(mirrored, 2, 3).astype(jnp.float32)
    averaged = (summed * 0.5).astype(jnp.bfloat16)
    spread = lax.all_gather(averaged, "recv", axis=3, tiled=True)
    spread = spread.reshape(freqs, 2, block_rows, recv_count, shot_count, piece_len)
    panel = jnp.transpose(spread, (0, 1, 2, 4, 3, 5)).reshape(freqs, 2, block_rows, total)
    recv_index = lax.axis_index("recv")
    own_tile = lax.dynamic_slice_in_dim(panel, recv_index * col_width, col_width, 3)
    product = complex_product(
        panel, lax.all_gather(own_tile, "shot", axis=2, tiled=True), "fik,fkj->fij"
    )
    scale_factor = jnp.float32(float(NS) ** (-0.5))
    return product * scale_factor


def solution(mesh):
    placed = (P(None, None, "shot", "recv"),)
    fits = mesh.shape["shot"] == 8 and mesh.shape["recv"] == 4
    return jax.shard_map(
        cube_per_device if fits else per_device,
        mesh=mesh,
        in_specs=placed,
        out_specs=P(None, None, "shot", "recv"),
        check_vma=False,
    )
```
